512 devices in a mesh: dual: 16 (over x, z_hi, core), primal: 8 (over y), seq: 4 (over z_lo).
Axes of the slice: x: 4, y: 8, z: 8 (z_hi: 2, z_lo: 4; z = z_hi * 4 + z_lo), core: 2. Of those that a mesh axis runs over, the one named last changes fastest.
Arguments:
- payoff: bfloat16 [16384, 16384], P('dual', 'primal'), may hold values from -0.0625 to 0.0625
- opp_strategy: float32 [16384, 1024], P(('primal', 'dual'), 'seq'), may hold values from 0 to 1
- opp_combos: int32 [16384], P(('primal', 'dual')), may hold values from 1 to 6
- seq_payoff: bfloat16 [1024, 1024], P(None, 'seq')
- seq_parent: int32 [1024], replicated, may hold values from 0 to 255, as said below
Outputs:
- strategy: float32 [16384, 1024], P(('dual', 'primal'), 'seq')
- opp_grad: float32 [16384, 1024], P(('primal', 'dual'), 'seq')
The draws below stay inside these ranges and needn't reach their ends.
Inputs may be any that keep to these rules, and one draw needn't show every extreme that they name: `seq_parent`: every information set 0 to 255 is left by at least one sequence.
All inputs are finite; a program needn't handle non-finite values. Where the reference program divides by a largest or mean magnitude, that divisor is 1e-20 or more.
Results may differ from the reference program's by a relative error of at most 0.01.
Values may be sent and summed in bfloat16 or wider, within the bound.
No kernel may reach another device: no remote copies, remote signals or barrier semaphores. Data moves between devices by JAX's collectives and lax.ppermute only.
A program may use at most 64 MiB of HBM per device.

```python
import math
import jax
import jax.numpy as jnp
from jax import lax

NB_P = 16384
NB_D = 16384
NS = 1024
NI = 256


def draw_seq_payoff(key, part):
    k_scale, k_base = jax.random.split(jax.random.fold_in(key, 7), 2)
    row_scale = jnp.exp(jax.random.uniform(k_scale, (NS, 1), jnp.float32) * math.log(10.0))
    base = jax.random.truncated_normal(k_base, -4.0, 4.0, (NS, NS), jnp.float32)
    return (base * row_scale / math.sqrt(NS)).astype(jnp.bfloat16)


def draw_seq_parent(key, part):
    k_fill, k_order = jax.random.split(jax.random.fold_in(key, 13))
    extra = jax.random.randint(k_fill, (NS - NI,), 0, NI, dtype=jnp.int32)
    labels = jnp.concatenate([jnp.arange(NI, dtype=jnp.int32), extra])
    return labels[jax.random.permutation(k_order, NS)]


def set_ends(drawn, key, least, high):
    index_at = [jax.random.randint(jax.random.fold_in(key, axis), (), 0, length) for axis, length in enumerate(drawn.shape)]
    main_axis = drawn.shape.index(max(drawn.shape))
    next_to = index_at[:main_axis] + [(index_at[main_axis] + 1) % drawn.shape[main_axis]] + index_at[main_axis + 1:]
    return drawn.at[tuple(index_at)].set(least).at[tuple(next_to)].set(high)


def strengthened(result, own_key, source, target, blocks, factor):
    owner, partner = [(jnp.arange(result.shape[position]) // (result.shape[position] // blocks)).reshape([-1 if axis == position else 1 for axis in range(result.ndim)]) for position in (source, target)]
    chosen = jax.random.permutation(own_key, blocks)[partner]
    strong = (owner == chosen) | (owner == (partner + blocks // 2) % blocks)
    return jnp.where(strong, factor * result, result)


def steps_of(own_key, extent, shards, least, high):
    loudness = 1.0
    for axis_at, parts in shards:
        steps = jax.random.uniform(jax.random.fold_in(jax.random.fold_in(own_key, 6), axis_at), (parts,), jnp.float32, least / len(shards), high / len(shards))
        loudness = loudness * jnp.repeat(jnp.exp(steps), extent[axis_at] // parts).reshape((-1,) + (1,) * (len(extent) - 1 - axis_at))
    return loudness


def heavy_noise(own_key, shape, deviation, reach, shards, heavy, kind=jnp.bfloat16):
    drawn = deviation * jax.random.normal(own_key, shape, jnp.float32)
    if shards:
        drawn = drawn * steps_of(own_key, shape, shards, -0.22, 0.18)
    return jnp.clip(strengthened(drawn, jax.random.fold_in(own_key, 3), *heavy), -reach, reach).astype(kind)


def setup_inputs(seed: int = 0) -> dict:
    splits = jax.random.split(jax.random.key(seed), 6)
    return {
        "payoff": heavy_noise(splits[0], (NB_P, NB_D), NB_D ** -0.5, 0.0625, ((0, 16), (1, 8)), (0, 1, 16, 2.0)),
        "opp_strategy": jnp.clip(1.0 * jax.random.uniform(splits[1], (NB_D, NS), jnp.float32) ** steps_of(splits[1], (NB_D, NS), ((0, 128), (1, 4)), -0.2, 0.2), 0.0, 1.0),
        "opp_combos": set_ends(jax.random.randint(splits[2], (NB_D,), 1, 7), jax.random.fold_in(splits[2], 1), 1, 6).astype(jnp.int32),
        "seq_payoff": draw_seq_payoff(jax.random.fold_in(splits[5], 71), 0),
        "seq_parent": draw_seq_parent(jax.random.fold_in(splits[5], 71), 0),
    }


logit_span = 6.0
epsilon = 1e-6


def reference(payoff, opp_strategy, opp_combos, seq_payoff, seq_parent):
    scaled = (opp_combos.astype(jnp.float32)[:, None] * opp_strategy).astype(jnp.bfloat16)
    inner_sum = jnp.dot(payoff, scaled, preferred_element_type=jnp.float32)
    inner_low = inner_sum.astype(jnp.bfloat16)
    gradient = jnp.dot(inner_low, seq_payoff.T, preferred_element_type=jnp.float32)
    largest = jnp.max(jnp.abs(gradient), axis=1)
    exponent = jnp.exp(-logit_span * gradient / (largest[:, None] + epsilon))
    onehot = (seq_parent[:, None] == jnp.arange(NI, dtype=jnp.int32)[None, :]).astype(jnp.float32)
    totals = jnp.dot(exponent, onehot, precision=lax.Precision.HIGHEST)
    strategy = exponent / jnp.dot(totals, onehot.T, precision=lax.Precision.HIGHEST)
    through = jnp.dot(strategy.astype(jnp.bfloat16), seq_payoff, preferred_element_type=jnp.float32).astype(jnp.bfloat16)
    opp_grad = jnp.dot(payoff.T, through, preferred_element_type=jnp.float32)
    return strategy, opp_grad
```

```python
import jax
import jax.numpy as jnp
from jax import lax
from jax.sharding import Mesh, PartitionSpec as P

logit_span = 6.0
epsilon = 1e-06

bf16 = jnp.bfloat16
f32 = jnp.float32
DUAL = ("x", "zh", "core")
SWAP = ((0, 1), (1, 0))


def exchange(blocks, axis):
    return lax.all_to_all(blocks, axis, split_axis=0, concat_axis=0, tiled=True)


def spread(block, copies, axis):
    return exchange(jnp.broadcast_to(block[None], (copies, *block.shape)), axis)


def pick(pair, index):
    return lax.dynamic_index_in_dim(pair, index, 0, keepdims=False)


def body(payoff, opp_strategy, opp_combos, seq_payoff, seq_parent):
    rows, width = opp_strategy.shape
    n_x, n_zh, n_y, n_seq = (lax.axis_size(a) for a in ("x", "zh", "primal", "seq"))
    core, zh, seq = (lax.axis_index(a) for a in ("core", "zh", "seq"))
    same = (seq_parent[:, None] == seq_parent[None, :]).astype(bf16)

    scaled = (opp_combos.astype(f32)[:, None] * opp_strategy).astype(bf16)
    part = jnp.einsum(
        "bt,zst->zbs",
        scaled,
        seq_payoff.reshape(n_seq, width, width),
        preferred_element_type=f32,
    ).astype(bf16)
    part = jnp.broadcast_to(part[None], (n_zh, *part.shape)).reshape(-1, rows, width)
    part = exchange(part, ("zh", "seq")).reshape(n_zh, n_seq, rows, width)
    mixed = part.astype(f32).sum(axis=1).astype(bf16)

    mixed = spread(mixed, n_x, "x").reshape(n_x * n_zh, rows, width)
    other = lax.ppermute(mixed, "core", SWAP)
    block = jnp.stack(
        [jnp.where(core == 0, mixed, other), jnp.where(core == 0, other, mixed)], axis=1
    ).reshape(-1, width)

    partial_grad = jnp.dot(payoff, block, preferred_element_type=f32).astype(bf16)
    partial_grad = exchange(partial_grad.reshape(n_y, rows, width), "primal")
    gradient = partial_grad.astype(f32).sum(axis=0).astype(bf16)
    gradient = spread(gradient, n_seq, "seq").astype(f32)

    largest = jnp.max(jnp.abs(gradient), axis=(0, 2), keepdims=True)
    exponent = jnp.exp(-logit_span * gradient / (largest + epsilon))
    exponent = jnp.swapaxes(exponent, 0, 1).reshape(rows, n_seq * width)
    high = exponent.astype(bf16)
    low = (exponent - high.astype(f32)).astype(bf16)
    totals = jnp.dot(
        jnp.concatenate([high, low], axis=0), same, preferred_element_type=f32
    )
    strategy = exponent / (totals[:rows] + totals[rows:])
    through = jnp.dot(
        strategy.astype(bf16), seq_payoff, preferred_element_type=f32
    ).astype(bf16)
    own_strategy = lax.dynamic_slice_in_dim(strategy, seq * width, width, 1)

    player_block = spread(through, n_y, "primal").reshape(-1, width)
    opp = lax.dot_general(
        payoff, player_block, (((0,), (0,)), ((), ())), preferred_element_type=f32
    ).astype(bf16)
    opp = opp.reshape(n_x * n_zh, 2, rows, width).swapaxes(0, 1)
    opp = pick(opp, core).astype(f32) + lax.ppermute(
        pick(opp, 1 - core), "core", SWAP
    ).astype(f32)
    opp = exchange(opp.astype(bf16).reshape(n_x, n_zh * rows, width), "x")
    opp = opp.astype(f32).sum(axis=0).reshape(n_zh, rows, width)
    opp_grad = pick(opp, zh) + lax.ppermute(
        pick(opp, 1 - zh).astype(bf16), "zh", SWAP
    ).astype(f32)
    return own_strategy, opp_grad


def solution(mesh):
    n_dual, n_primal, n_seq = mesh.devices.shape
    fine = Mesh(
        mesh.devices.reshape(n_dual // 4, 2, 2, n_primal, n_seq),
        (*DUAL, "primal", "seq"),
    )
    opponent_rows = ("primal", *DUAL)
    return jax.shard_map(
        body,
        mesh=fine,
        in_specs=(
            P(DUAL, "primal"),
            P(opponent_rows, "seq"),
            P(opponent_rows),
            P(None, "seq"),
            P(),
        ),
        out_specs=(P((*DUAL, "primal"), "seq"), P(opponent_rows, "seq")),
        check_vma=False,
    )
```

```python
import jax
import jax.numpy as jnp
from jax import lax
from jax.experimental import pallas as pl
from jax.experimental.pallas import tpu as pltpu
from jax.sharding import Mesh, PartitionSpec as P

logit_span = 6.0
epsilon = 1e-06

bf16 = jnp.bfloat16
f32 = jnp.float32
DUAL = ("x", "zh", "core")
CHIPS = ("x", "zh")
PLANE = ("primal", "seq")
SWAP = ((0, 1), (1, 0))


def exchange(blocks, axis):
    return lax.all_to_all(blocks, axis, split_axis=0, concat_axis=0, tiled=True)


def spread(block, copies, axis):
    return exchange(jnp.broadcast_to(block[None], (copies, *block.shape)), axis)


def pick(pair, index):
    return lax.dynamic_index_in_dim(pair, index, 0, keepdims=False)


def player_kernel(payoff_ref, block_ref, out_ref):
    out_ref[...] = jnp.dot(
        payoff_ref[...], block_ref[...], preferred_element_type=f32
    ).astype(bf16)


def player_product(payoff, block):
    n_rows, depth = payoff.shape
    width = block.shape[1]
    step = n_rows // 4
    return pl.pallas_call(
        player_kernel,
        grid=(n_rows // step,),
        in_specs=[
            pl.BlockSpec((step, depth), lambda i: (i, 0)),
            pl.BlockSpec((depth, width), lambda i: (0, 0)),
        ],
        out_specs=pl.BlockSpec((step, width), lambda i: (i, 0)),
        out_shape=jax.ShapeDtypeStruct((n_rows, width), bf16),
        cost_estimate=pl.CostEstimate(
            flops=2 * n_rows * depth * width,
            bytes_accessed=2 * n_rows * depth,
            transcendentals=0,
        ),
    )(payoff, block)


def opponent_kernel(payoff_ref, block_ref, out_ref, turned):
    @pl.when(pl.program_id(0) == 0)
    def _():
        turned[...] = block_ref[...].T

    total = jnp.dot(turned[...], payoff_ref[...], preferred_element_type=f32)
    rows = out_ref.shape[-1]
    for chip in range(out_ref.shape[1]):
        for core in range(2):
            at = (2 * chip + core) * rows
            out_ref[core, chip] = total[:, at : at + rows].astype(bf16)


def opponent_product(payoff, block, chips, rows):
    depth, n_cols = payoff.shape
    width = block.shape[1]
    step = 2
    return pl.pallas_call(
        opponent_kernel,
        grid=(chips // step,),
        in_specs=[
            pl.BlockSpec((depth, step * 2 * rows), lambda i: (0, i)),
            pl.BlockSpec((depth, width), lambda i: (0, 0)),
        ],
        out_specs=pl.BlockSpec((2, step, width, rows), lambda i: (0, i, 0, 0)),
        out_shape=jax.ShapeDtypeStruct((2, chips, width, rows), bf16),
        scratch_shapes=[pltpu.VMEM((width, depth), bf16)],
        cost_estimate=pl.CostEstimate(
            flops=2 * n_cols * depth * width,
            bytes_accessed=2 * n_cols * depth,
            transcendentals=0,
        ),
    )(payoff, block)


def body(payoff, opp_strategy, opp_combos, seq_payoff, seq_parent):
    rows, width = opp_strategy.shape
    n_chip = lax.axis_size(CHIPS)
    n_y, n_seq = lax.axis_size("primal"), lax.axis_size("seq")
    core, seq = lax.axis_index("core"), lax.axis_index("seq")
    part_rows = rows // n_seq
    n_all = n_seq * width
    whole_payoff = lax.all_gather(seq_payoff, "seq", axis=1, tiled=True)
    same = (seq_parent[:, None] == seq_parent[None, :]).astype(bf16)

    scaled = (opp_combos.astype(f32)[:, None] * opp_strategy).astype(bf16)
    scaled = spread(scaled, n_chip, CHIPS).reshape(n_chip, rows, width)
    other = lax.ppermute(scaled, "core", SWAP)
    block = jnp.stack(
        [jnp.where(core == 0, scaled, other), jnp.where(core == 0, other, scaled)],
        axis=1,
    ).reshape(-1, width)

    inner = player_product(payoff, block).reshape(n_y * n_seq, part_rows, width)
    inner = exchange(inner, PLANE).reshape(n_y, n_seq, part_rows, width)
    inner = inner.astype(f32).sum(axis=0).astype(bf16)
    inner = jnp.swapaxes(inner, 0, 1).reshape(part_rows, n_all)
    gradient = lax.dot_general(
        inner, whole_payoff, (((1,), (1,)), ((), ())), preferred_element_type=f32
    )

    largest = jnp.max(jnp.abs(gradient), axis=1, keepdims=True)
    exponent = jnp.exp(-logit_span * gradient / (largest + epsilon))
    high = exponent.astype(bf16)
    low = (exponent - high.astype(f32)).astype(bf16)
    totals = jnp.dot(
        jnp.concatenate([high, low], axis=0), same, preferred_element_type=f32
    )
    strategy = exponent / (totals[:part_rows] + totals[part_rows:])
    through = jnp.dot(
        strategy.astype(bf16), whole_payoff, preferred_element_type=f32
    ).astype(bf16)

    through = jnp.swapaxes(through.reshape(part_rows, n_seq, width), 0, 1)
    through = jnp.broadcast_to(through[None], (n_y, *through.shape))
    player_block = exchange(through.reshape(n_y * n_seq, part_rows, width), PLANE)

    strategy = jnp.swapaxes(strategy.reshape(part_rows, n_seq, width), 0, 1)
    own_strategy = jnp.zeros((n_seq, part_rows, width), f32)
    for hop in range(n_seq):
        piece = pick(strategy, (seq + hop) % n_seq)
        if hop:
            piece = lax.ppermute(
                piece, "seq", [(i, (i + hop) % n_seq) for i in range(n_seq)]
            )
        own_strategy = lax.dynamic_update_index_in_dim(
            own_strategy, piece, (seq - hop) % n_seq, 0
        )
    own_strategy = own_strategy.reshape(rows, width)

    opp = opponent_product(payoff, player_block.reshape(-1, width), n_chip, rows)
    opp = pick(opp, core).astype(f32) + lax.ppermute(
        pick(opp, 1 - core), "core", SWAP
    ).astype(f32)
    opp = exchange(opp.astype(bf16), CHIPS)
    opp_grad = opp.astype(f32).sum(axis=0).T
    return own_strategy, opp_grad


def solution(mesh):
    n_dual, n_primal, n_seq = mesh.devices.shape
    fine = Mesh(
        mesh.devices.reshape(n_dual // 4, 2, 2, n_primal, n_seq),
        (*DUAL, *PLANE),
    )
    opponent_rows = ("primal", *DUAL)
    return jax.shard_map(
        body,
        mesh=fine,
        in_specs=(
            P(DUAL, "primal"),
            P(opponent_rows, "seq"),
            P(opponent_rows),
            P(None, "seq"),
            P(),
        ),
        out_specs=(P((*DUAL, "primal"), "seq"), P(opponent_rows, "seq")),
        check_vma=False,
    )
```

```python
import jax
import jax.numpy as jnp
from jax import lax
from jax.sharding import Mesh, PartitionSpec as P

logit_span = 6.0
epsilon = 1e-06

bf16 = jnp.bfloat16
f32 = jnp.float32
DUAL = ("x", "zh", "core")
PLANE = ("primal", "seq")
LINE = ("zh", "seq")
SWAP = ((0, 1), (1, 0))


def exchange(blocks, axis):
    return lax.all_to_all(blocks, axis, split_axis=0, concat_axis=0, tiled=True)


def spread(block, copies, axis):
    return exchange(jnp.broadcast_to(block[None], (copies, *block.shape)), axis)


def swap(block, axis):
    return lax.ppermute(block, axis, SWAP)


def shift(block, axis, hop):
    size = lax.axis_size(axis)
    return lax.ppermute(block, axis, [(i, (i + hop) % size) for i in range(size)])


def pick(stack, index):
    return lax.dynamic_index_in_dim(stack, index, 0, keepdims=False)


def in_order(first, own, other, axis):
    return jnp.stack(
        [jnp.where(first, own, other), jnp.where(first, other, own)], axis=axis
    )


def body(payoff, opp_strategy, opp_combos, seq_payoff, seq_parent):
    rows, width = opp_strategy.shape
    n_x, n_y, n_seq = (lax.axis_size(a) for a in ("x", "primal", "seq"))
    zh, core, seq = (lax.axis_index(a) for a in ("zh", "core", "seq"))
    part_rows = rows // n_seq
    n_all = n_seq * width
    half = n_all // 2
    same = (seq_parent[:, None] == seq_parent[None, :]).astype(bf16)

    scaled = (opp_combos.astype(f32)[:, None] * opp_strategy).astype(bf16)
    far = swap(scaled, "zh")
    near = spread(scaled, n_x, "x").reshape(n_x, rows, width)
    near_other = swap(near, "core")

    own_half = lax.dynamic_slice_in_dim(seq_payoff, core * half, half, 0)
    quarter = half // 2
    behind = shift(own_half, LINE, 1)
    ahead = shift(own_half, LINE, -1)
    across = jnp.concatenate(
        [shift(own_half[:quarter], LINE, 2), shift(own_half[quarter:], LINE, -2)],
        axis=0,
    )

    far = spread(far, n_x, "x").reshape(n_x, rows, width)
    far, ahead, across, behind = lax.optimization_barrier((far, ahead, across, behind))
    far_other = swap(far, "core")
    near = in_order(core == 0, near, near_other, 1)
    far = in_order(core == 0, far, far_other, 1)
    block = in_order(zh == 0, near, far, 1).reshape(-1, width)

    fetched = jnp.stack([ahead, across, behind])
    fetched_other = swap(fetched, "core")
    fetched = in_order(core == 0, fetched, fetched_other, 1).reshape(-1, n_all, width)
    whole = jnp.concatenate([seq_payoff[None], fetched], axis=0)

    inner = jnp.dot(payoff, block, preferred_element_type=f32).astype(bf16)
    inner = exchange(inner.reshape(n_y * n_seq, part_rows, width), PLANE)
    inner = inner.reshape(n_y, n_seq, part_rows, width).astype(f32).sum(axis=0)
    inner = inner.astype(bf16)
    gradient = sum(
        lax.dot_general(
            pick(inner, (seq + hop) % n_seq),
            whole[hop],
            (((1,), (1,)), ((), ())),
            preferred_element_type=f32,
        )
        for hop in range(n_seq)
    )

    largest = jnp.max(jnp.abs(gradient), axis=1, keepdims=True)
    exponent = jnp.exp(-logit_span * gradient / (largest + epsilon))
    high = exponent.astype(bf16)
    low = (exponent - high.astype(f32)).astype(bf16)
    totals = jnp.dot(
        jnp.concatenate([high, low], axis=0), same, preferred_element_type=f32
    )
    strategy = exponent / (totals[:part_rows] + totals[part_rows:])
    strategy_low = strategy.astype(bf16)
    through = jnp.stack(
        [
            jnp.dot(strategy_low, whole[hop], preferred_element_type=f32).astype(bf16)
            for hop in range(n_seq)
        ]
    )
    through = jnp.stack([pick(through, (i - seq) % n_seq) for i in range(n_seq)])
    through = jnp.broadcast_to(through[None], (n_y, *through.shape))
    player_block = exchange(through.reshape(n_y * n_seq, part_rows, width), PLANE)

    strategy = jnp.stack(jnp.split(strategy, n_seq, axis=1))
    own_strategy = jnp.zeros((n_seq, part_rows, width), f32)
    for hop in range(n_seq):
        piece = pick(strategy, (seq + hop) % n_seq)
        if hop:
            piece = shift(piece, "seq", hop)
        own_strategy = lax.dynamic_update_index_in_dim(
            own_strategy, piece, (seq - hop) % n_seq, 0
        )
    own_strategy, player_block = lax.optimization_barrier((own_strategy, player_block))
    own_strategy = own_strategy.reshape(rows, width)

    opp = lax.dot_general(
        player_block.reshape(-1, width),
        payoff,
        (((0,), (0,)), ((), ())),
        preferred_element_type=f32,
    ).astype(bf16)
    opp = opp.reshape(width, n_x, 2, 2, rows).transpose(2, 3, 1, 0, 4)

    def over_cores(pair):
        return (
            pick(pair, core).astype(f32)
            + swap(pick(pair, 1 - core), "core").astype(f32)
        ).astype(bf16)

    far = exchange(over_cores(pick(opp, 1 - zh)), "x")
    near = over_cores(pick(opp, zh))
    far, near = lax.optimization_barrier((far, near))
    far = swap(far.astype(f32).sum(axis=0).astype(bf16), "zh")
    near = exchange(near, "x").astype(f32).sum(axis=0)
    return own_strategy, (near + far.astype(f32)).T


def solution(mesh):
    n_dual, n_primal, n_seq = mesh.devices.shape
    fine = Mesh(
        mesh.devices.reshape(n_dual // 4, 2, 2, n_primal, n_seq),
        (*DUAL, *PLANE),
    )
    opponent_rows = ("primal", *DUAL)
    return jax.shard_map(
        body,
        mesh=fine,
        in_specs=(
            P(DUAL, "primal"),
            P(opponent_rows, "seq"),
            P(opponent_rows),
            P(None, "seq"),
            P(),
        ),
        out_specs=(P((*DUAL, "primal"), "seq"), P(opponent_rows, "seq")),
        check_vma=False,
    )
```

```python
import jax
import jax.numpy as jnp
from jax import lax
from jax.experimental import pallas as pl
from jax.experimental.pallas import tpu as pltpu
from jax.sharding import Mesh, PartitionSpec as P

logit_span = 6.0
epsilon = 1e-06

bf16 = jnp.bfloat16
f32 = jnp.float32
DUAL = ("x", "zh", "core")
KERNEL_VMEM = 16 << 20
SWAP = ((0, 1), (1, 0))


def exchange(blocks, axis):
    return lax.all_to_all(blocks, axis, split_axis=0, concat_axis=0, tiled=True)


def spread(block, copies, axis):
    return exchange(jnp.broadcast_to(block[None], (copies, *block.shape)), axis)


def pick(pair, first):
    return jnp.where(first, pair[0], pair[1])


def resident(array):
    return pltpu.with_memory_space_constraint(array, pltpu.VMEM)


VMEM_SPEC = pl.BlockSpec(memory_space=pltpu.VMEM)


def player_kernel(payoff_ref, block_ref, out_ref):
    step = 256

    @pl.loop(0, payoff_ref.shape[0] // step)
    def _(i):
        at = pl.ds(pl.multiple_of(i * step, step), step)
        out_ref[at, :] = jnp.dot(
            payoff_ref[at, :], block_ref[...], preferred_element_type=f32
        ).astype(bf16)


def player_product(payoff, block):
    n_rows, depth = payoff.shape
    width = block.shape[1]
    return pl.pallas_call(
        player_kernel,
        in_specs=[VMEM_SPEC] * 2,
        out_specs=VMEM_SPEC,
        out_shape=jax.ShapeDtypeStruct((n_rows, width), bf16),
        compiler_params=pltpu.CompilerParams(vmem_limit_bytes=KERNEL_VMEM),
        cost_estimate=pl.CostEstimate(
            flops=2 * n_rows * depth * width,
            bytes_accessed=2 * n_rows * depth,
            transcendentals=0,
        ),
    )(resident(payoff), block)


def opponent_kernel(payoff_ref, block_ref, out_ref, turned):
    turned[...] = block_ref[...].T
    chips, width, rows = out_ref.shape[1:]

    @pl.loop(0, chips)
    def _(chip):
        at = pl.ds(pl.multiple_of(chip * 2 * rows, 2 * rows), 2 * rows)
        total = jnp.dot(
            turned[...], payoff_ref[:, at], preferred_element_type=f32
        ).astype(bf16)
        out_ref[0, chip] = total[:, :rows]
        out_ref[1, chip] = total[:, rows:]


def opponent_product(payoff, block, chips, rows):
    depth, n_cols = payoff.shape
    width = block.shape[1]
    return pl.pallas_call(
        opponent_kernel,
        in_specs=[VMEM_SPEC] * 2,
        out_specs=VMEM_SPEC,
        out_shape=jax.ShapeDtypeStruct((2, chips, width, rows), bf16),
        scratch_shapes=[pltpu.VMEM((width, depth), bf16)],
        compiler_params=pltpu.CompilerParams(vmem_limit_bytes=KERNEL_VMEM),
        cost_estimate=pl.CostEstimate(
            flops=2 * n_cols * depth * width,
            bytes_accessed=2 * n_cols * depth,
            transcendentals=0,
        ),
    )(resident(payoff), block)


def body(payoff, opp_strategy, opp_combos, seq_payoff, seq_parent):
    rows, width = opp_strategy.shape
    n_x, n_zh, n_y, n_seq = (lax.axis_size(a) for a in ("x", "zh", "primal", "seq"))
    core, zh, seq = (lax.axis_index(a) for a in ("core", "zh", "seq"))
    core_first, zh_first = core == 0, zh == 0
    core_second, zh_second = core == 1, zh == 1
    same = (seq_parent[:, None] == seq_parent[None, :]).astype(bf16)

    scaled = (opp_combos.astype(f32)[:, None] * opp_strategy).astype(bf16)
    part = jnp.einsum(
        "bt,zst->zbs",
        scaled,
        seq_payoff.reshape(n_seq, width, width),
        preferred_element_type=f32,
    ).astype(bf16)
    part = jnp.broadcast_to(part[None], (n_zh, *part.shape)).reshape(-1, rows, width)
    part = exchange(part, ("zh", "seq")).reshape(n_zh, n_seq, rows, width)
    mixed = part.astype(f32).sum(axis=1).astype(bf16)

    mixed = spread(mixed, n_x, "x").reshape(n_x * n_zh, rows, width)
    other = lax.ppermute(mixed, "core", SWAP)

    block = jnp.stack(
        [jnp.where(core_first, mixed, other), jnp.where(core_first, other, mixed)],
        axis=1,
    )
    partial_grad = player_product(payoff, block.reshape(-1, width))
    own_at = (seq * width).astype(jnp.uint32)
    partial_grad, own_at, core_first, core_second, zh_first, zh_second = (
        lax.optimization_barrier(
            (partial_grad, own_at, core_first, core_second, zh_first, zh_second)
        )
    )
    partial_grad = exchange(partial_grad.reshape(n_y, rows, width), "primal")
    gradient = partial_grad.astype(f32).sum(axis=0).astype(bf16)
    gradient = spread(gradient, n_seq, "seq").astype(f32)

    largest = jnp.max(jnp.abs(gradient), axis=(0, 2), keepdims=True)
    exponent = jnp.exp(-logit_span * gradient / (largest + epsilon))
    exponent = jnp.swapaxes(exponent, 0, 1).reshape(rows, n_seq * width)
    high = exponent.astype(bf16)
    low = (exponent - high.astype(f32)).astype(bf16)
    totals = jnp.dot(
        jnp.concatenate([high, low], axis=0), same, preferred_element_type=f32
    )
    strategy = exponent / (totals[:rows] + totals[rows:])
    through = jnp.dot(
        strategy.astype(bf16), seq_payoff, preferred_element_type=f32
    ).astype(bf16)
    own_strategy = lax.dynamic_slice(
        strategy, (jnp.uint32(0), own_at), (rows, width)
    )

    player_block = spread(through, n_y, "primal").reshape(-1, width)
    opp = opponent_product(payoff, player_block, n_x * n_zh, rows)
    opp = pick(opp, core_first).astype(f32) + lax.ppermute(
        pick(opp, core_second), "core", SWAP
    ).astype(f32)
    opp = exchange(opp.astype(bf16).reshape(n_x, n_zh * width, rows), "x")
    opp = opp.astype(f32).sum(axis=0).reshape(n_zh, width, rows)
    opp_grad = pick(opp, zh_first) + lax.ppermute(
        pick(opp, zh_second).astype(bf16), "zh", SWAP
    ).astype(f32)
    opp_grad = opp_grad.T
    return own_strategy, opp_grad


def solution(mesh):
    n_dual, n_primal, n_seq = mesh.devices.shape
    fine = Mesh(
        mesh.devices.reshape(n_dual // 4, 2, 2, n_primal, n_seq),
        (*DUAL, "primal", "seq"),
    )
    opponent_rows = ("primal", *DUAL)
    return jax.shard_map(
        body,
        mesh=fine,
        in_specs=(
            P(DUAL, "primal"),
            P(opponent_rows, "seq"),
            P(opponent_rows),
            P(None, "seq"),
            P(),
        ),
        out_specs=(P((*DUAL, "primal"), "seq"), P(opponent_rows, "seq")),
        check_vma=False,
    )
```

```python
import jax
import jax.numpy as jnp
from jax import lax
from jax.experimental import pallas as pl
from jax.experimental.pallas import tpu as pltpu
from jax.sharding import Mesh, PartitionSpec as P

logit_span = 6.0
epsilon = 1e-06

bf16 = jnp.bfloat16
f32 = jnp.float32
DUAL = ("x", "zh", "core")
KERNEL_VMEM = 16 << 20
PLANE = ("primal", "seq")
LINE = ("zh", "seq")
SWAP = ((0, 1), (1, 0))


def exchange(blocks, axis):
    return lax.all_to_all(blocks, axis, split_axis=0, concat_axis=0, tiled=True)


def spread(block, copies, axis):
    return exchange(jnp.broadcast_to(block[None], (copies, *block.shape)), axis)


def pick(pair, first):
    return jnp.where(first, pair[0], pair[1])


def resident(array):
    return pltpu.with_memory_space_constraint(array, pltpu.VMEM)


VMEM_SPEC = pl.BlockSpec(memory_space=pltpu.VMEM)


def player_kernel(payoff_ref, block_ref, out_ref):
    step = 256

    @pl.loop(0, payoff_ref.shape[0] // step)
    def _(i):
        at = pl.ds(pl.multiple_of(i * step, step), step)
        out_ref[at, :] = jnp.dot(
            payoff_ref[at, :], block_ref[...], preferred_element_type=f32
        ).astype(bf16)


def player_product(payoff, block):
    n_rows, depth = payoff.shape
    width = block.shape[1]
    return pl.pallas_call(
        player_kernel,
        in_specs=[VMEM_SPEC] * 2,
        out_specs=VMEM_SPEC,
        out_shape=jax.ShapeDtypeStruct((n_rows, width), bf16),
        compiler_params=pltpu.CompilerParams(vmem_limit_bytes=KERNEL_VMEM),
        cost_estimate=pl.CostEstimate(
            flops=2 * n_rows * depth * width,
            bytes_accessed=2 * n_rows * depth,
            transcendentals=0,
        ),
    )(resident(payoff), block)


def opponent_kernel(payoff_ref, block_ref, out_ref, turned):
    turned[...] = block_ref[...].T
    chips, width, rows = out_ref.shape[1:]

    @pl.loop(0, chips)
    def _(chip):
        at = pl.ds(pl.multiple_of(chip * 2 * rows, 2 * rows), 2 * rows)
        total = jnp.dot(
            turned[...], payoff_ref[:, at], preferred_element_type=f32
        ).astype(bf16)
        out_ref[0, chip] = total[:, :rows]
        out_ref[1, chip] = total[:, rows:]


def opponent_product(payoff, block, chips, rows):
    depth, n_cols = payoff.shape
    width = block.shape[1]
    return pl.pallas_call(
        opponent_kernel,
        in_specs=[VMEM_SPEC] * 2,
        out_specs=VMEM_SPEC,
        out_shape=jax.ShapeDtypeStruct((2, chips, width, rows), bf16),
        scratch_shapes=[pltpu.VMEM((width, depth), bf16)],
        compiler_params=pltpu.CompilerParams(vmem_limit_bytes=KERNEL_VMEM),
        cost_estimate=pl.CostEstimate(
            flops=2 * n_cols * depth * width,
            bytes_accessed=2 * n_cols * depth,
            transcendentals=0,
        ),
    )(resident(payoff), block)


def body(payoff, opp_strategy, opp_combos, seq_payoff, seq_parent):
    rows, width = opp_strategy.shape
    n_x, n_zh, n_y, n_seq = (lax.axis_size(a) for a in ("x", "zh", "primal", "seq"))
    core = lax.axis_index("core")
    core_first, core_second = core == 0, core == 1
    part_rows = rows // n_seq
    same = (seq_parent[:, None] == seq_parent[None, :]).astype(bf16)

    scaled = (opp_combos.astype(f32)[:, None] * opp_strategy).astype(bf16)
    part = jnp.einsum(
        "bt,zst->zbs",
        scaled,
        seq_payoff.reshape(n_seq, width, width),
        preferred_element_type=f32,
    ).astype(bf16)
    part = jnp.broadcast_to(part[None], (n_zh, *part.shape)).reshape(-1, rows, width)
    part = exchange(part, LINE).reshape(n_zh, n_seq, rows, width)
    mixed = part.astype(f32).sum(axis=1).astype(bf16)

    mixed = spread(mixed, n_x, "x").reshape(n_x * n_zh, rows, width)
    other = lax.ppermute(mixed, "core", SWAP)

    block = jnp.stack(
        [jnp.where(core_first, mixed, other), jnp.where(core_first, other, mixed)],
        axis=1,
    )
    partial_grad = player_product(payoff, block.reshape(-1, width))
    own_y = lax.axis_index("primal").astype(jnp.uint32)
    partial_grad, own_y, core_first, core_second = lax.optimization_barrier(
        (partial_grad, own_y, core_first, core_second)
    )
    partial_grad = exchange(
        partial_grad.reshape(n_y * n_seq, part_rows, width), PLANE
    ).reshape(n_y, n_seq, part_rows, width)
    gradient = partial_grad.astype(f32).sum(axis=0)

    largest = jnp.max(jnp.abs(gradient), axis=(0, 2), keepdims=True)
    exponent = jnp.exp(-logit_span * gradient / (largest + epsilon))
    exponent = jnp.swapaxes(exponent, 0, 1).reshape(part_rows, n_seq * width)
    high = exponent.astype(bf16)
    low = (exponent - high.astype(f32)).astype(bf16)
    totals = jnp.dot(
        jnp.concatenate([high, low], axis=0), same, preferred_element_type=f32
    )
    strategy = (exponent / (totals[:part_rows] + totals[part_rows:])).astype(bf16)
    strategy = jnp.swapaxes(strategy.reshape(part_rows, n_seq, width), 0, 1)
    strategy = jnp.broadcast_to(strategy[None], (n_y, *strategy.shape))
    strategy = exchange(strategy.reshape(n_y * n_seq, part_rows, width), PLANE)
    strategy = strategy.reshape(n_y, rows, width)
    own_strategy = lax.dynamic_index_in_dim(strategy, own_y, 0, False).astype(f32)

    opp = opponent_product(payoff, strategy.reshape(-1, width), n_x * n_zh, rows)
    opp = pick(opp, core_first).astype(f32) + lax.ppermute(
        pick(opp, core_second), "core", SWAP
    ).astype(f32)
    opp, own_strategy = lax.optimization_barrier((opp.astype(bf16), own_strategy))
    opp = exchange(opp.reshape(n_x, n_zh * width, rows), "x")
    opp = opp.astype(f32).sum(axis=0).astype(bf16).reshape(n_zh, 1, width, rows)
    opp = jnp.broadcast_to(opp, (n_zh, n_seq, width, rows))
    opp = exchange(opp.reshape(n_zh * n_seq, width, rows), LINE)
    opp = opp.reshape(n_zh, n_seq * width, rows)
    opp = (opp[0].astype(f32) + opp[1].astype(f32)).astype(bf16)
    opp_grad = lax.dot_general(
        opp, seq_payoff, (((0,), (0,)), ((), ())), preferred_element_type=f32
    )
    return own_strategy, opp_grad


def solution(mesh):
    n_dual, n_primal, n_seq = mesh.devices.shape
    fine = Mesh(
        mesh.devices.reshape(n_dual // 4, 2, 2, n_primal, n_seq),
        (*DUAL, "primal", "seq"),
    )
    opponent_rows = ("primal", *DUAL)
    return jax.shard_map(
        body,
        mesh=fine,
        in_specs=(
            P(DUAL, "primal"),
            P(opponent_rows, "seq"),
            P(opponent_rows),
            P(None, "seq"),
            P(),
        ),
        out_specs=(P((*DUAL, "primal"), "seq"), P(opponent_rows, "seq")),
        check_vma=False,
    )
```

```python
import functools

import jax
import jax.numpy as jnp
from jax import lax
from jax.experimental import pallas as pl
from jax.experimental.pallas import tpu as pltpu
from jax.sharding import Mesh, PartitionSpec as P

logit_span = 6.0
epsilon = 1e-06

bf16 = jnp.bfloat16
f32 = jnp.float32
DUAL = ("x", "zh", "core")
NI = 256
KERNEL_VMEM = 16 << 20
SWAP = ((0, 1), (1, 0))


def exchange(blocks, axis):
    return lax.all_to_all(blocks, axis, split_axis=0, concat_axis=0, tiled=True)


def spread(block, copies, axis):
    return exchange(jnp.broadcast_to(block[None], (copies, *block.shape)), axis)


def pick(pair, first):
    return jnp.where(first, pair[0], pair[1])


def resident(array):
    return pltpu.with_memory_space_constraint(array, pltpu.VMEM)


VMEM_SPEC = pl.BlockSpec(memory_space=pltpu.VMEM)


def player_kernel(payoff_ref, block_ref, out_ref):
    step = 256

    @pl.loop(0, payoff_ref.shape[0] // step)
    def _(i):
        at = pl.ds(pl.multiple_of(i * step, step), step)
        out_ref[at, :] = jnp.dot(
            payoff_ref[at, :], block_ref[...], preferred_element_type=f32
        ).astype(bf16)


def player_product(payoff, block):
    n_rows, depth = payoff.shape
    width = block.shape[1]
    return pl.pallas_call(
        player_kernel,
        in_specs=[VMEM_SPEC] * 2,
        out_specs=VMEM_SPEC,
        out_shape=jax.ShapeDtypeStruct((n_rows, width), bf16),
        compiler_params=pltpu.CompilerParams(vmem_limit_bytes=KERNEL_VMEM),
        cost_estimate=pl.CostEstimate(
            flops=2 * n_rows * depth * width,
            bytes_accessed=2 * n_rows * depth,
            transcendentals=0,
        ),
    )(resident(payoff), block)


def opponent_kernel(core_ref, payoff_ref, block_ref, out_ref, turned):
    parts, _, part = block_ref.shape
    for i in range(parts):
        turned[:, i * part : (i + 1) * part] = block_ref[i]
    chips, _, rows = out_ref.shape
    core = core_ref[0]

    def strip(chip):
        at = pl.multiple_of((2 * chip + core) * rows, rows)
        return payoff_ref[:, pl.ds(at, rows)]

    @pl.loop(0, chips // 2)
    def _(i):
        total = jnp.dot(
            turned[...],
            jnp.concatenate([strip(2 * i), strip(2 * i + 1)], axis=1),
            preferred_element_type=f32,
        ).astype(bf16)
        out_ref[2 * i] = total[:, :rows]
        out_ref[2 * i + 1] = total[:, rows:]


def opponent_product(core, payoff, block, chips, rows):
    depth, n_cols = payoff.shape
    width = block.shape[1]
    return pl.pallas_call(
        opponent_kernel,
        in_specs=[pl.BlockSpec(memory_space=pltpu.SMEM)] + [VMEM_SPEC] * 2,
        out_specs=VMEM_SPEC,
        out_shape=jax.ShapeDtypeStruct((chips, width, rows), bf16),
        scratch_shapes=[pltpu.VMEM((width, depth), bf16)],
        compiler_params=pltpu.CompilerParams(vmem_limit_bytes=KERNEL_VMEM),
        cost_estimate=pl.CostEstimate(
            flops=n_cols * depth * width,
            bytes_accessed=n_cols * depth,
            transcendentals=0,
        ),
    )(core[None], resident(payoff), block)


def prox_kernel(
    seq_ref, gradient_ref, seq_payoff_ref, parent_ref, through_ref, own_ref, all_ref
):
    n_seq, rows, width = gradient_ref.shape
    gradient = [gradient_ref[i].astype(f32) for i in range(n_seq)]
    largest = functools.reduce(jnp.maximum, [jnp.abs(g) for g in gradient])
    largest = jnp.max(largest, axis=1, keepdims=True)
    exponent = jnp.exp(
        -logit_span * jnp.concatenate(gradient, axis=1) / (largest + epsilon)
    )

    def halves(value):
        high = value.astype(bf16)
        low = (value - high.astype(f32)).astype(bf16)
        return jnp.concatenate([high, low], axis=0)

    infosets = lax.broadcasted_iota(jnp.int32, (NI, n_seq * width), 0)
    member = (infosets == parent_ref[...]).astype(f32).astype(bf16)
    totals = lax.dot_general(
        halves(exponent), member, (((1,), (1,)), ((), ())), preferred_element_type=f32
    )
    totals = jnp.dot(
        halves(totals[:rows] + totals[rows:]), member, preferred_element_type=f32
    )
    strategy = exponent / (totals[:rows] + totals[rows:])
    for i in range(n_seq):
        all_ref[i] = strategy[:, i * width : (i + 1) * width]
    own_ref[...] = all_ref[seq_ref[0]]
    through = jnp.dot(
        strategy.astype(bf16), seq_payoff_ref[...], preferred_element_type=f32
    )
    through = through.T.astype(bf16)
    for i in range(through_ref.shape[0]):
        through_ref[i] = through


def prox(seq, gradient, seq_payoff, seq_parent, copies):
    n_seq, rows, width = gradient.shape
    return pl.pallas_call(
        prox_kernel,
        in_specs=[pl.BlockSpec(memory_space=pltpu.SMEM)] + [VMEM_SPEC] * 3,
        out_specs=(VMEM_SPEC, VMEM_SPEC),
        out_shape=(
            jax.ShapeDtypeStruct((copies, width, rows), bf16),
            jax.ShapeDtypeStruct((rows, width), f32),
        ),
        scratch_shapes=[pltpu.VMEM((n_seq, rows, width), f32)],
        compiler_params=pltpu.CompilerParams(vmem_limit_bytes=KERNEL_VMEM),
        cost_estimate=pl.CostEstimate(
            flops=64 * n_seq * rows * width * NI,
            bytes_accessed=2 * seq_payoff.size,
            transcendentals=n_seq * rows * width,
        ),
    )(seq[None], gradient, seq_payoff, seq_parent[None])


def body(payoff, opp_strategy, opp_combos, seq_payoff, seq_parent):
    rows, width = opp_strategy.shape
    n_x, n_zh, n_y, n_seq = (lax.axis_size(a) for a in ("x", "zh", "primal", "seq"))
    core, zh, seq = (lax.axis_index(a) for a in ("core", "zh", "seq"))
    core_first, zh_first = core == 0, zh == 0
    zh_second = zh == 1

    scaled = (opp_combos.astype(f32)[:, None] * opp_strategy).astype(bf16)
    part = jnp.einsum(
        "bt,zst->zbs",
        scaled,
        seq_payoff.reshape(n_seq, width, width),
        preferred_element_type=f32,
    ).astype(bf16)
    part = jnp.broadcast_to(part[None], (n_zh, *part.shape)).reshape(-1, rows, width)
    part = exchange(part, ("zh", "seq")).reshape(n_zh, n_seq, rows, width)
    mixed = part.astype(f32).sum(axis=1).astype(bf16)

    mixed = spread(mixed, n_x, "x").reshape(n_x * n_zh, rows, width)
    other = lax.ppermute(mixed, "core", SWAP)

    block = jnp.stack(
        [jnp.where(core_first, mixed, other), jnp.where(core_first, other, mixed)],
        axis=1,
    )
    partial_grad = player_product(payoff, block.reshape(-1, width))
    partial_grad, core, mate, seq, zh_first, zh_second = lax.optimization_barrier(
        (partial_grad, core, 1 - core, seq, zh_first, zh_second)
    )
    partial_grad = exchange(partial_grad.reshape(n_y, rows, width), "primal")
    gradient = partial_grad.astype(f32).sum(axis=0).astype(bf16)
    gradient = spread(gradient, n_seq, "seq")
    through, own_strategy = prox(seq, gradient, seq_payoff, seq_parent, n_y)

    through = exchange(through, "primal")
    away = opponent_product(mate, payoff, through, n_x * n_zh, rows)
    away = lax.ppermute(away, "core", SWAP)
    opp = opponent_product(core, payoff, through, n_x * n_zh, rows)
    opp = opp.astype(f32) + away.astype(f32)
    opp = exchange(opp.astype(bf16).reshape(n_x, n_zh * width, rows), "x")
    opp = opp.astype(f32).sum(axis=0).reshape(n_zh, width, rows)
    opp_grad = pick(opp, zh_first) + lax.ppermute(
        pick(opp, zh_second).astype(bf16), "zh", SWAP
    ).astype(f32)
    opp_grad = opp_grad.T
    return own_strategy, opp_grad


def solution(mesh):
    n_dual, n_primal, n_seq = mesh.devices.shape
    fine = Mesh(
        mesh.devices.reshape(n_dual // 4, 2, 2, n_primal, n_seq),
        (*DUAL, "primal", "seq"),
    )
    opponent_rows = ("primal", *DUAL)
    return jax.shard_map(
        body,
        mesh=fine,
        in_specs=(
            P(DUAL, "primal"),
            P(opponent_rows, "seq"),
            P(opponent_rows),
            P(None, "seq"),
            P(),
        ),
        out_specs=(P((*DUAL, "primal"), "seq"), P(opponent_rows, "seq")),
        check_vma=False,
    )
```

```python
import functools

import jax
import jax.numpy as jnp
from jax import lax
from jax.experimental import pallas as pl
from jax.experimental.pallas import tpu as pltpu
from jax.sharding import Mesh, PartitionSpec as P

logit_span = 6.0
epsilon = 1e-06

bf16 = jnp.bfloat16
f32 = jnp.float32
DUAL = ("x", "zh", "core")
NI = 256
KERNEL_VMEM = 16 << 20
SWAP = ((0, 1), (1, 0))


def exchange(blocks, axis):
    return lax.all_to_all(blocks, axis, split_axis=0, concat_axis=0, tiled=True)


def spread(block, copies, axis):
    return exchange(jnp.broadcast_to(block[None], (copies, *block.shape)), axis)


def pick(pair, first):
    return jnp.where(first, pair[0], pair[1])


def resident(array):
    return pltpu.with_memory_space_constraint(array, pltpu.VMEM)


VMEM_SPEC = pl.BlockSpec(memory_space=pltpu.VMEM)


def player_kernel(payoff_ref, block_ref, out_ref):
    step = 256

    @pl.loop(0, payoff_ref.shape[0] // step)
    def _(i):
        at = pl.ds(pl.multiple_of(i * step, step), step)
        out_ref[at, :] = jnp.dot(
            payoff_ref[at, :], block_ref[...], preferred_element_type=f32
        ).astype(bf16)


def player_product(payoff, block):
    n_rows, depth = payoff.shape
    width = block.shape[1]
    return pl.pallas_call(
        player_kernel,
        in_specs=[VMEM_SPEC] * 2,
        out_specs=VMEM_SPEC,
        out_shape=jax.ShapeDtypeStruct((n_rows, width), bf16),
        compiler_params=pltpu.CompilerParams(vmem_limit_bytes=KERNEL_VMEM),
        cost_estimate=pl.CostEstimate(
            flops=2 * n_rows * depth * width,
            bytes_accessed=2 * n_rows * depth,
            transcendentals=0,
        ),
    )(resident(payoff), block)


def opponent_kernel(core_ref, payoff_ref, block_ref, out_ref, turned):
    parts, _, part = block_ref.shape
    for i in range(parts):
        turned[:, i * part : (i + 1) * part] = block_ref[i]
    _, chips, _, rows = out_ref.shape
    core = core_ref[0]

    def strip(chip):
        at = pl.multiple_of((2 * chip + core) * rows, rows)
        return payoff_ref[:, pl.ds(at, rows)]

    @pl.loop(0, chips)
    def _(i):
        total = jnp.dot(
            turned[...],
            jnp.concatenate([strip(2 * i), strip(2 * i + 1)], axis=1),
            preferred_element_type=f32,
        ).astype(bf16)
        out_ref[0, i] = total[:, :rows]
        out_ref[1, i] = total[:, rows:]


def opponent_product(core, payoff, block, chips, rows):
    depth, n_cols = payoff.shape
    width = block.shape[1]
    return pl.pallas_call(
        opponent_kernel,
        in_specs=[pl.BlockSpec(memory_space=pltpu.SMEM)] + [VMEM_SPEC] * 2,
        out_specs=VMEM_SPEC,
        out_shape=jax.ShapeDtypeStruct((2, chips // 2, width, rows), bf16),
        scratch_shapes=[pltpu.VMEM((width, depth), bf16)],
        compiler_params=pltpu.CompilerParams(vmem_limit_bytes=KERNEL_VMEM),
        cost_estimate=pl.CostEstimate(
            flops=n_cols * depth * width,
            bytes_accessed=n_cols * depth,
            transcendentals=0,
        ),
    )(core[None], resident(payoff), block)


def prox_kernel(
    seq_ref, gradient_ref, seq_payoff_ref, parent_ref, through_ref, own_ref, all_ref
):
    n_seq, rows, width = gradient_ref.shape
    gradient = [gradient_ref[i].astype(f32) for i in range(n_seq)]
    largest = functools.reduce(jnp.maximum, [jnp.abs(g) for g in gradient])
    largest = jnp.max(largest, axis=1, keepdims=True)
    exponent = jnp.exp(
        -logit_span * jnp.concatenate(gradient, axis=1) / (largest + epsilon)
    )

    def halves(value):
        high = value.astype(bf16)
        low = (value - high.astype(f32)).astype(bf16)
        return jnp.concatenate([high, low], axis=0)

    infosets = lax.broadcasted_iota(jnp.int32, (NI, n_seq * width), 0)
    member = (infosets == parent_ref[...]).astype(f32).astype(bf16)
    totals = lax.dot_general(
        halves(exponent), member, (((1,), (1,)), ((), ())), preferred_element_type=f32
    )
    totals = jnp.dot(
        halves(totals[:rows] + totals[rows:]), member, preferred_element_type=f32
    )
    strategy = exponent / (totals[:rows] + totals[rows:])
    for i in range(n_seq):
        all_ref[i] = strategy[:, i * width : (i + 1) * width]
    own_ref[...] = all_ref[seq_ref[0]]
    through = jnp.dot(
        strategy.astype(bf16), seq_payoff_ref[...], preferred_element_type=f32
    )
    through = through.T.astype(bf16)
    for i in range(through_ref.shape[0]):
        through_ref[i] = through


def prox(seq, gradient, seq_payoff, seq_parent, copies):
    n_seq, rows, width = gradient.shape
    return pl.pallas_call(
        prox_kernel,
        in_specs=[pl.BlockSpec(memory_space=pltpu.SMEM)] + [VMEM_SPEC] * 3,
        out_specs=(VMEM_SPEC, VMEM_SPEC),
        out_shape=(
            jax.ShapeDtypeStruct((copies, width, rows), bf16),
            jax.ShapeDtypeStruct((rows, width), f32),
        ),
        scratch_shapes=[pltpu.VMEM((n_seq, rows, width), f32)],
        compiler_params=pltpu.CompilerParams(vmem_limit_bytes=KERNEL_VMEM),
        cost_estimate=pl.CostEstimate(
            flops=64 * n_seq * rows * width * NI,
            bytes_accessed=2 * seq_payoff.size,
            transcendentals=n_seq * rows * width,
        ),
    )(seq[None], gradient, seq_payoff, seq_parent[None])


def body(payoff, opp_strategy, opp_combos, seq_payoff, seq_parent):
    rows, width = opp_strategy.shape
    n_x, n_zh, n_y, n_seq = (lax.axis_size(a) for a in ("x", "zh", "primal", "seq"))
    core, zh, seq = (lax.axis_index(a) for a in ("core", "zh", "seq"))
    core_first, zh_first = core == 0, zh == 0
    zh_second = zh == 1

    scaled = (opp_combos.astype(f32)[:, None] * opp_strategy).astype(bf16)
    part = jnp.einsum(
        "bt,zst->zbs",
        scaled,
        seq_payoff.reshape(n_seq, width, width),
        preferred_element_type=f32,
    ).astype(bf16)
    part = jnp.broadcast_to(part[None], (n_zh, *part.shape)).reshape(-1, rows, width)
    part = exchange(part, ("zh", "seq")).reshape(n_zh, n_seq, rows, width)
    mixed = part.astype(f32).sum(axis=1).astype(bf16)

    mixed = spread(mixed, n_x, "x").reshape(n_x * n_zh, rows, width)
    other = lax.ppermute(mixed, "core", SWAP)

    block = jnp.stack(
        [jnp.where(core_first, mixed, other), jnp.where(core_first, other, mixed)],
        axis=1,
    )
    partial_grad = player_product(payoff, block.reshape(-1, width))
    partial_grad, core, mate, seq, zh_first, zh_second = lax.optimization_barrier(
        (partial_grad, core, 1 - core, seq, zh_first, zh_second)
    )
    partial_grad = exchange(partial_grad.reshape(n_y, rows, width), "primal")
    gradient = partial_grad.astype(f32).sum(axis=0).astype(bf16)
    gradient = spread(gradient, n_seq, "seq")
    through, own_strategy = prox(seq, gradient, seq_payoff, seq_parent, n_y)

    through = exchange(through, "primal")
    away = opponent_product(mate, payoff, through, n_x * n_zh, rows)
    away = lax.ppermute(away, "core", SWAP)
    opp = opponent_product(core, payoff, through, n_x * n_zh, rows)
    opp = (opp.astype(f32) + away.astype(f32)).astype(bf16)
    far = exchange(pick(opp, zh_second), "x")
    far, near = lax.optimization_barrier((far, pick(opp, zh_first)))
    far = lax.ppermute(far.astype(f32).sum(axis=0).astype(bf16), "zh", SWAP)
    near = exchange(near, "x").astype(f32).sum(axis=0)
    return own_strategy, (near + far.astype(f32)).T


def solution(mesh):
    n_dual, n_primal, n_seq = mesh.devices.shape
    fine = Mesh(
        mesh.devices.reshape(n_dual // 4, 2, 2, n_primal, n_seq),
        (*DUAL, "primal", "seq"),
    )
    opponent_rows = ("primal", *DUAL)
    return jax.shard_map(
        body,
        mesh=fine,
        in_specs=(
            P(DUAL, "primal"),
            P(opponent_rows, "seq"),
            P(opponent_rows),
            P(None, "seq"),
            P(),
        ),
        out_specs=(P((*DUAL, "primal"), "seq"), P(opponent_rows, "seq")),
        check_vma=False,
    )
```
